32 devices in a mesh: layer: 4 (over z), row: 8 (over y, x, core).
Axes of the slice: x: 2, y: 2, z: 4, core: 2. Of those that a mesh axis runs over, the one named last changes fastest.
Arguments:
- rhs_sub: float32 [4, 3, 4096, 256], P('layer', None, 'row'), may hold values from -6 to 6
- rhs_root: float32 [2048, 256], P('row'), may hold values from -6 to 6
- lower_inv: float32 [4, 3, 4096, 4096], P('layer', None, 'row'), may hold values from -0.09375 to 0.09375
- upper_inv: float32 [4, 3, 4096, 4096], P('layer', None, 'row'), may hold values from -0.09375 to 0.09375
- coupling_low: float32 [4, 3, 2048, 4096], P('layer', None, None, 'row'), may hold values from -0.0390625 to 0.0390625
- coupling_up: float32 [4, 3, 4096, 2048], P('layer', None, 'row'), may hold values from -0.1875 to 0.1875
- tile_mask: int32 [4, 3, 16, 32], P('layer', None, None, 'row'), may hold values 0 or 1
- root_inv: float32 [2048, 2048], P('row'), may hold values from -0.125 to 0.125
Outputs:
- sol_sub: float32 [4, 3, 4096, 256], P('layer', None, 'row')
- sol_root: float32 [2048, 256], P('row')
The draws below stay inside these ranges and needn't reach their ends.
All inputs are finite; a program needn't handle non-finite values. No bound on the sum of `tile_mask` on one device may be relied on, other than what follows from the above.
Results may differ from the reference program's by a relative error of at most 0.0001.
Values sent between devices are 32-bit elements; how exact they have to be, the bound alone decides.
A program may use at most 192 MiB of HBM per device.

```python
import jax
import jax.numpy as jnp
from jax import lax

S = 4096
NA = 2048
TILE = 128
NSUP = 3
NRHS = 256
LAYERS = 4


def set_ends(result, own_key, least, high):
    extent = result.shape
    index_at = [jax.random.randint(jax.random.fold_in(own_key, axis), (), 0, extent[axis]) for axis in range(len(extent))]
    result = result.at[tuple(index_at)].set(least)
    longest = extent.index(max(extent))
    index_at[longest] = (index_at[longest] + 1) % extent[longest]
    return result.at[tuple(index_at)].set(high)


def shard_levels(key, extent, cuts, low, top_value):
    loudness = 1.0
    for axis_at, blocks in cuts:
        heights = jax.random.uniform(jax.random.fold_in(jax.random.fold_in(key, 6), axis_at), (blocks,), jnp.float32, low / len(cuts), top_value / len(cuts))
        loudness = loudness * jnp.repeat(jnp.exp(heights), extent[axis_at] // blocks).reshape((-1,) + (1,) * (len(extent) - 1 - axis_at))
    return loudness


def scatter_about(own_key, extent, spread, bound, cuts=(), held_as=jnp.bfloat16):
    values = spread * jax.random.normal(own_key, extent, jnp.float32)
    if cuts:
        values = values * shard_levels(own_key, extent, cuts, -0.22, 0.18)
    return jnp.clip(values, -bound, bound).astype(held_as)


def setup_inputs(seed: int = 0) -> dict:
    streams_of = jax.random.split(jax.random.key(seed), 9)
    return {
        "rhs_sub": scatter_about(streams_of[0], (LAYERS, NSUP, S, NRHS), 1.0, 6.0, ((0, 4), (2, 8)), jnp.float32),
        "rhs_root": scatter_about(streams_of[1], (NA, NRHS), 1.0, 6.0, ((0, 8),), jnp.float32),
        "lower_inv": scatter_about(streams_of[2], (LAYERS, NSUP, S, S), S ** -0.5, 0.09375, ((0, 4), (2, 8)), jnp.float32),
        "upper_inv": scatter_about(streams_of[3], (LAYERS, NSUP, S, S), S ** -0.5, 0.09375, ((0, 4), (2, 8)), jnp.float32),
        "coupling_low": scatter_about(streams_of[4], (LAYERS, NSUP, NA, S), (S * NSUP * LAYERS // 2) ** -0.5, 0.0390625, ((0, 4), (3, 8)), jnp.float32),
        "coupling_up": scatter_about(streams_of[5], (LAYERS, NSUP, S, NA), (NA // 2) ** -0.5, 0.1875, ((0, 4), (2, 8)), jnp.float32),
        "tile_mask": set_ends((jax.random.randint(streams_of[6], (LAYERS, NSUP, NA // TILE, S // TILE), 0, 2) < 1).astype(jnp.int32), jax.random.fold_in(streams_of[6], 1), 0, 1),
        "root_inv": scatter_about(streams_of[7], (NA, NA), NA ** -0.5, 0.125, ((0, 8),), jnp.float32),
    }


def masked_tiles(coupling, pattern, tile, flipped):
    blocks, height, breadth = coupling.shape
    shaped = coupling.reshape(blocks, height // tile, tile, breadth // tile, tile)
    if flipped:
        pattern = jnp.transpose(pattern, (0, 2, 1))
    weights = pattern.astype(jnp.float32)[:, :, None, :, None]
    return (shaped * weights).reshape(blocks, height, breadth)


def reference(rhs_sub, rhs_root, lower_inv, upper_inv, coupling_low, coupling_up, tile_mask, root_inv):
    highest = lax.Precision.HIGHEST
    interims = []
    total = jnp.zeros(rhs_root.shape, jnp.float32)
    for layer in range(LAYERS):
        row_list = []
        for block in range(NSUP):
            interim = jnp.dot(lower_inv[layer, block], rhs_sub[layer, block], precision=highest, preferred_element_type=jnp.float32)
            weights = masked_tiles(coupling_low[layer, block][None], tile_mask[layer, block][None], TILE, False)[0]
            total = total + jnp.dot(weights, interim, precision=highest, preferred_element_type=jnp.float32)
            row_list.append(interim)
        interims.append(row_list)
    reduced = rhs_root - total
    sol_root = jnp.dot(root_inv, reduced, precision=highest, preferred_element_type=jnp.float32)
    layer_list = []
    for layer in range(LAYERS):
        row_list = []
        for block in range(NSUP):
            weights = masked_tiles(coupling_up[layer, block][None], tile_mask[layer, block][None], TILE, True)[0]
            residue = interims[layer][block] - jnp.dot(weights, sol_root, precision=highest, preferred_element_type=jnp.float32)
            row_list.append(jnp.dot(upper_inv[layer, block], residue, precision=highest, preferred_element_type=jnp.float32))
        layer_list.append(jnp.stack(row_list))
    return jnp.stack(layer_list), sol_root
```

```python
import functools

import jax
import jax.numpy as jnp
from jax import lax
from jax.experimental import pallas as pl
from jax.experimental.pallas import tpu as pltpu
from jax.sharding import PartitionSpec as P

TILE = 128
CUBE = 8
MESH = pl.DeviceIdType.MESH
F32, BF16 = jnp.float32, jnp.bfloat16


def split(a):
    high = a.astype(BF16)
    return high, (a - high.astype(F32)).astype(BF16)


def dot3(a, b):
    ah, al = split(a)
    bh, bl = split(b)
    dot = functools.partial(jnp.dot, preferred_element_type=F32)
    return dot(ah, bh) + (dot(ah, bl) + dot(al, bh))


def gather_kernel(multiply, *refs):
    if multiply:
        x_ref, w_hbm, out_ref, held, weights, send_sem, recv_sem, w_sem = refs
    else:
        x_ref, out_ref, send_sem, recv_sem = refs
        held = out_ref
    count, depth, _ = x_ref.shape
    half = depth // 2
    me = lax.axis_index("row")
    layer = lax.axis_index("layer")
    core = lax.rem(me, 2)
    ax = lax.rem(me // 2, 2)
    ay = me // 4

    def place(fy, fx, fc):
        y = 1 - ay if fy else ay
        x = 1 - ax if fx else ax
        c = 1 - core if fc else core
        return y * 4 + x * 2 + c

    own, sib, xn, yn = place(0, 0, 0), place(0, 0, 1), place(0, 1, 0), place(1, 0, 0)
    diag, sx, sy, sd = place(1, 1, 0), place(0, 1, 1), place(1, 0, 1), place(1, 1, 1)

    barrier = pltpu.get_barrier_semaphore()
    for to in (sib, xn, yn):
        pl.semaphore_signal(barrier, inc=1, device_id=(layer, to), device_id_type=MESH)

    def weight_copy(k):
        return pltpu.make_async_copy(w_hbm.at[k], weights.at[k], w_sem.at[k])

    if multiply:
        for k in range(count):
            weight_copy(k).start()
    for k in range(count):
        held[k, own] = x_ref[k]
    pl.semaphore_wait(barrier, 3)

    low, high = pl.ds(0, half), pl.ds(half, half)
    routes = (
        (own, None, sib),
        (own, None, xn),
        (own, None, yn),
        (xn, low, yn),
        (xn, None, sib),
        (yn, high, xn),
        (yn, None, sib),
        (diag, low, sib),
        (diag, high, sib),
    )

    def route(slot, k):
        block, rows, to = routes[slot]
        ref = held.at[k, block] if rows is None else held.at[k, block, rows]
        return pltpu.make_async_remote_copy(
            src_ref=ref,
            dst_ref=ref,
            send_sem=send_sem.at[slot, k],
            recv_sem=recv_sem.at[slot, k],
            device_id=(layer, to),
            device_id_type=MESH,
        )

    def meet(k, block):
        if multiply:
            columns = pl.ds(pl.multiple_of(block * depth, depth), depth)
            out_ref[k] += dot3(weights[k, :, columns], held[k, block])

    for k in range(count):
        for slot in (1, 2, 0):
            route(slot, k).start()

    def first(k, carry):
        if multiply:
            weight_copy(k).wait()
            out_ref[k] = jnp.zeros(out_ref.shape[1:], F32)
            meet(k, own)
        return carry

    def second(k, carry):
        route(1, k).wait_recv()
        route(3, k).start()
        route(4, k).start()
        route(2, k).wait_recv()
        route(5, k).start()
        route(6, k).start()
        meet(k, xn)
        meet(k, yn)
        route(0, k).wait_recv()
        meet(k, sib)
        return carry

    def third(k, carry):
        route(3, k).wait_recv()
        route(7, k).start()
        route(5, k).wait_recv()
        route(8, k).start()
        route(4, k).wait_recv()
        meet(k, sx)
        route(6, k).wait_recv()
        meet(k, sy)
        meet(k, diag)
        route(7, k).wait_recv()
        route(8, k).wait_recv()
        meet(k, sd)
        return carry

    def last(k, carry):
        for slot in range(9):
            route(slot, k).wait_send()
        return carry

    for stage in (first, second, third, last):
        lax.fori_loop(0, count, stage, 0)


def gather_multiply(matrices, piece, collective_id):
    count, rows, wide = matrices.shape
    _, depth, breadth = piece.shape
    return pl.pallas_call(
        functools.partial(gather_kernel, True),
        out_shape=jax.ShapeDtypeStruct((count, rows, breadth), F32),
        in_specs=[pl.BlockSpec(memory_space=pltpu.VMEM), pl.BlockSpec(memory_space=pl.ANY)],
        out_specs=pl.BlockSpec(memory_space=pltpu.VMEM),
        scratch_shapes=[
            pltpu.VMEM((count, CUBE, depth, breadth), F32),
            pltpu.VMEM((count, rows, wide), F32),
            pltpu.SemaphoreType.DMA((9, count)),
            pltpu.SemaphoreType.DMA((9, count)),
            pltpu.SemaphoreType.DMA((count,)),
        ],
        compiler_params=pltpu.CompilerParams(
            collective_id=collective_id, has_side_effects=True, vmem_limit_bytes=56 << 20
        ),
        cost_estimate=pl.CostEstimate(
            flops=6 * count * rows * wide * breadth, bytes_accessed=4 * matrices.size, transcendentals=0
        ),
    )(piece, matrices)


def gather_only(piece, collective_id):
    depth, breadth = piece.shape
    out = pl.pallas_call(
        functools.partial(gather_kernel, False),
        out_shape=jax.ShapeDtypeStruct((1, CUBE, depth, breadth), F32),
        in_specs=[pl.BlockSpec(memory_space=pltpu.VMEM)],
        out_specs=pl.BlockSpec(memory_space=pltpu.VMEM),
        scratch_shapes=[pltpu.SemaphoreType.DMA((9, 1)), pltpu.SemaphoreType.DMA((9, 1))],
        compiler_params=pltpu.CompilerParams(
            collective_id=collective_id, has_side_effects=True, vmem_limit_bytes=16 << 20
        ),
    )(piece[None])
    return out.reshape(CUBE * depth, breadth)


def low_kernel(c_ref, m_ref, x_ref, o_ref):
    k = pl.program_id(1)

    @pl.when(k == 0)
    def _():
        o_ref[...] = jnp.zeros_like(o_ref)

    for t in range(c_ref.shape[1] // TILE):
        rows = pl.ds(t * TILE, TILE)
        o_ref[rows, :] += dot3(c_ref[0, rows, :] * m_ref[0, t], x_ref[k])


def masked_low(coupling, pattern, interim):
    count, height, wide = coupling.shape
    breadth = interim.shape[2]
    block = min(512, height)
    weights = jnp.repeat(pattern.astype(F32), TILE, axis=2)[:, :, None, :]
    return pl.pallas_call(
        low_kernel,
        grid=(height // block, count),
        out_shape=jax.ShapeDtypeStruct((height, breadth), F32),
        in_specs=[
            pl.BlockSpec((1, block, wide), lambda i, k: (k, i, 0)),
            pl.BlockSpec((1, block // TILE, 1, wide), lambda i, k: (k, i, 0, 0)),
            pl.BlockSpec(interim.shape, lambda i, k: (0, 0, 0)),
        ],
        out_specs=pl.BlockSpec((block, breadth), lambda i, k: (i, 0)),
        compiler_params=pltpu.CompilerParams(vmem_limit_bytes=32 << 20),
    )(coupling, weights, interim)


def up_kernel(u_ref, m_ref, s_ref, i_ref, o_ref):
    for t in range(u_ref.shape[1] // TILE):
        rows = pl.ds(t * TILE, TILE)
        o_ref[0, rows, :] = i_ref[0, rows, :] - dot3(u_ref[0, rows, :] * m_ref[0, t], s_ref[...])


def masked_up(coupling, pattern, sol_root, interim):
    count, height, wide = coupling.shape
    breadth = sol_root.shape[1]
    block = min(256, height)
    weights = jnp.repeat(jnp.transpose(pattern, (0, 2, 1)).astype(F32), TILE, axis=2)[:, :, None, :]
    return pl.pallas_call(
        up_kernel,
        grid=(count, height // block),
        out_shape=jax.ShapeDtypeStruct((count, height, breadth), F32),
        in_specs=[
            pl.BlockSpec((1, block, wide), lambda k, i: (k, i, 0)),
            pl.BlockSpec((1, block // TILE, 1, wide), lambda k, i: (k, i, 0, 0)),
            pl.BlockSpec(sol_root.shape, lambda k, i: (0, 0)),
            pl.BlockSpec((1, block, breadth), lambda k, i: (k, i, 0)),
        ],
        out_specs=pl.BlockSpec((1, block, breadth), lambda k, i: (k, i, 0)),
        compiler_params=pltpu.CompilerParams(vmem_limit_bytes=32 << 20),
    )(coupling, weights, sol_root, interim)


def fold(cube, matrices, piece, collective_id):
    if cube:
        return gather_multiply(matrices, piece, collective_id)
    whole = lax.all_gather(piece, "row", axis=1, tiled=True)
    return jnp.einsum("kij,kjr->kir", matrices, whole, precision=lax.Precision.HIGHEST)


def body(cube, rhs_sub, rhs_root, lower_inv, upper_inv, coupling_low, coupling_up, tile_mask, root_inv):
    pattern = tile_mask[0]
    interim = fold(cube, lower_inv[0], rhs_sub[0], 1)
    partial = masked_low(coupling_low[0], pattern, interim)
    partial = lax.psum_scatter(partial, "row", scatter_dimension=0, tiled=True)
    reduced = rhs_root - lax.psum(partial, "layer")
    sol_root = fold(cube, root_inv[None], reduced[None], 2)[0]
    if cube:
        whole = gather_only(sol_root, 3)
    else:
        whole = lax.all_gather(sol_root, "row", axis=0, tiled=True)
    residue = masked_up(coupling_up[0], pattern, whole, interim)
    solved = fold(cube, upper_inv[0], residue, 4)
    return solved[None], sol_root


def solution(mesh):
    return jax.shard_map(
        functools.partial(body, mesh.shape["row"] == CUBE),
        mesh=mesh,
        in_specs=(
            P("layer", None, "row", None),
            P("row", None),
            P("layer", None, "row", None),
            P("layer", None, "row", None),
            P("layer", None, None, "row"),
            P("layer", None, "row", None),
            P("layer", None, None, "row"),
            P("row", None),
        ),
        out_specs=(P("layer", None, "row", None), P("row", None)),
        check_vma=False,
    )
```

```python
import functools

import jax
import jax.numpy as jnp
from jax import lax
from jax.experimental import pallas as pl
from jax.experimental.pallas import tpu as pltpu
from jax.sharding import PartitionSpec as P

TILE = 128
CUBE = 8
MESH = pl.DeviceIdType.MESH
F32, BF16 = jnp.float32, jnp.bfloat16


def split(a):
    high = a.astype(BF16)
    return high, (a - high.astype(F32)).astype(BF16)


def dot3(a, b):
    ah, al = split(a)
    bh, bl = split(b)
    dot = functools.partial(jnp.dot, preferred_element_type=F32)
    return dot(ah, bh) + (dot(ah, bl) + dot(al, bh))


def gather_kernel(multiply, *refs):
    if multiply:
        x_ref, w_hbm, out_ref, held, weights, send_sem, recv_sem, w_sem = refs
    else:
        x_ref, out_ref, send_sem, recv_sem = refs
        held = out_ref
    count, depth, _ = x_ref.shape
    half = depth // 2
    me = lax.axis_index("row")
    layer = lax.axis_index("layer")
    core = lax.rem(me, 2)
    ax = lax.rem(me // 2, 2)
    ay = me // 4

    def place(fy, fx, fc):
        y = 1 - ay if fy else ay
        x = 1 - ax if fx else ax
        c = 1 - core if fc else core
        return y * 4 + x * 2 + c

    own, sib, xn, yn = place(0, 0, 0), place(0, 0, 1), place(0, 1, 0), place(1, 0, 0)
    diag, sx, sy, sd = place(1, 1, 0), place(0, 1, 1), place(1, 0, 1), place(1, 1, 1)

    barrier = pltpu.get_barrier_semaphore()
    for to in (sib, xn, yn):
        pl.semaphore_signal(barrier, inc=1, device_id=(layer, to), device_id_type=MESH)

    def weight_copy(k):
        return pltpu.make_async_copy(w_hbm.at[k], weights.at[k], w_sem.at[k])

    if multiply:
        for k in range(count):
            weight_copy(k).start()
    for k in range(count):
        held[k, own] = x_ref[k]
    pl.semaphore_wait(barrier, 3)

    low, high = pl.ds(0, half), pl.ds(half, half)
    routes = (
        (own, None, sib),
        (own, None, xn),
        (own, None, yn),
        (xn, low, yn),
        (xn, None, sib),
        (yn, high, xn),
        (yn, None, sib),
        (diag, low, sib),
        (diag, high, sib),
    )

    def route(slot, k):
        block, rows, to = routes[slot]
        ref = held.at[k, block] if rows is None else held.at[k, block, rows]
        return pltpu.make_async_remote_copy(
            src_ref=ref,
            dst_ref=ref,
            send_sem=send_sem.at[slot, k],
            recv_sem=recv_sem.at[slot, k],
            device_id=(layer, to),
            device_id_type=MESH,
        )

    def meet(k, block):
        if multiply:
            columns = pl.ds(pl.multiple_of(block * depth, depth), depth)
            out_ref[k] += dot3(weights[k, :, columns], held[k, block])

    for k in range(count):
        for slot in (1, 2, 0):
            route(slot, k).start()

    def first(k, carry):
        if multiply:
            weight_copy(k).wait()
            out_ref[k] = jnp.zeros(out_ref.shape[1:], F32)
            meet(k, own)
        return carry

    def second(k, carry):
        route(1, k).wait_recv()
        route(3, k).start()
        route(4, k).start()
        route(2, k).wait_recv()
        route(5, k).start()
        route(6, k).start()
        meet(k, xn)
        meet(k, yn)
        route(0, k).wait_recv()
        meet(k, sib)
        return carry

    def third(k, carry):
        route(3, k).wait_recv()
        route(7, k).start()
        route(5, k).wait_recv()
        route(8, k).start()
        route(4, k).wait_recv()
        meet(k, sx)
        route(6, k).wait_recv()
        meet(k, sy)
        meet(k, diag)
        route(7, k).wait_recv()
        route(8, k).wait_recv()
        meet(k, sd)
        return carry

    def last(k, carry):
        for slot in range(9):
            route(slot, k).wait_send()
        return carry

    for stage in (first, second, third, last):
        lax.fori_loop(0, count, stage, 0)


def gather_multiply(matrices, piece, collective_id):
    count, rows, wide = matrices.shape
    _, depth, breadth = piece.shape
    return pl.pallas_call(
        functools.partial(gather_kernel, True),
        out_shape=jax.ShapeDtypeStruct((count, rows, breadth), F32),
        in_specs=[pl.BlockSpec(memory_space=pltpu.VMEM), pl.BlockSpec(memory_space=pl.ANY)],
        out_specs=pl.BlockSpec(memory_space=pltpu.VMEM),
        scratch_shapes=[
            pltpu.VMEM((count, CUBE, depth, breadth), F32),
            pltpu.VMEM((count, rows, wide), F32),
            pltpu.SemaphoreType.DMA((9, count)),
            pltpu.SemaphoreType.DMA((9, count)),
            pltpu.SemaphoreType.DMA((count,)),
        ],
        compiler_params=pltpu.CompilerParams(
            collective_id=collective_id, has_side_effects=True, vmem_limit_bytes=56 << 20
        ),
        cost_estimate=pl.CostEstimate(
            flops=6 * count * rows * wide * breadth, bytes_accessed=4 * matrices.size, transcendentals=0
        ),
    )(piece, matrices)


def gather_only(piece, collective_id):
    depth, breadth = piece.shape
    out = pl.pallas_call(
        functools.partial(gather_kernel, False),
        out_shape=jax.ShapeDtypeStruct((1, CUBE, depth, breadth), F32),
        in_specs=[pl.BlockSpec(memory_space=pltpu.VMEM)],
        out_specs=pl.BlockSpec(memory_space=pltpu.VMEM),
        scratch_shapes=[pltpu.SemaphoreType.DMA((9, 1)), pltpu.SemaphoreType.DMA((9, 1))],
        compiler_params=pltpu.CompilerParams(
            collective_id=collective_id, has_side_effects=True, vmem_limit_bytes=16 << 20
        ),
    )(piece[None])
    return out.reshape(CUBE * depth, breadth)


def low_kernel(c_ref, m_ref, x_ref, o_ref):
    k = pl.program_id(1)

    @pl.when(k == 0)
    def _():
        o_ref[...] = jnp.zeros_like(o_ref)

    for t in range(c_ref.shape[1] // TILE):
        rows = pl.ds(t * TILE, TILE)
        o_ref[rows, :] += dot3(c_ref[0, rows, :] * m_ref[0, t], x_ref[k])


def masked_low(coupling, pattern, interim):
    count, height, wide = coupling.shape
    breadth = interim.shape[2]
    block = min(512, height)
    weights = jnp.repeat(pattern.astype(F32), TILE, axis=2)[:, :, None, :]
    return pl.pallas_call(
        low_kernel,
        grid=(height // block, count),
        out_shape=jax.ShapeDtypeStruct((height, breadth), F32),
        in_specs=[
            pl.BlockSpec((1, block, wide), lambda i, k: (k, i, 0)),
            pl.BlockSpec((1, block // TILE, 1, wide), lambda i, k: (k, i, 0, 0)),
            pl.BlockSpec(interim.shape, lambda i, k: (0, 0, 0)),
        ],
        out_specs=pl.BlockSpec((block, breadth), lambda i, k: (i, 0)),
        compiler_params=pltpu.CompilerParams(vmem_limit_bytes=32 << 20),
    )(coupling, weights, interim)


def up_kernel(u_ref, m_ref, s_ref, i_ref, o_ref):
    for t in range(u_ref.shape[1] // TILE):
        rows = pl.ds(t * TILE, TILE)
        o_ref[0, rows, :] = i_ref[0, rows, :] - dot3(u_ref[0, rows, :] * m_ref[0, t], s_ref[...])


def masked_up(coupling, pattern, sol_root, interim):
    count, height, wide = coupling.shape
    breadth = sol_root.shape[1]
    block = min(256, height)
    weights = jnp.repeat(jnp.transpose(pattern, (0, 2, 1)).astype(F32), TILE, axis=2)[:, :, None, :]
    return pl.pallas_call(
        up_kernel,
        grid=(count, height // block),
        out_shape=jax.ShapeDtypeStruct((count, height, breadth), F32),
        in_specs=[
            pl.BlockSpec((1, block, wide), lambda k, i: (k, i, 0)),
            pl.BlockSpec((1, block // TILE, 1, wide), lambda k, i: (k, i, 0, 0)),
            pl.BlockSpec(sol_root.shape, lambda k, i: (0, 0)),
            pl.BlockSpec((1, block, breadth), lambda k, i: (k, i, 0)),
        ],
        out_specs=pl.BlockSpec((1, block, breadth), lambda k, i: (k, i, 0)),
        compiler_params=pltpu.CompilerParams(vmem_limit_bytes=32 << 20),
    )(coupling, weights, sol_root, interim)


def reduce_kernel(layers, p_ref, rhs_ref, out_ref, from_sib, acc, from_x, from_y, mid_x, mid_y, end_x, end_y, total, from_z,
                  sib_sem, plane_sem, z_sem):
    depth = rhs_ref.shape[0]
    half = depth // 2
    piece = depth // layers
    me = lax.axis_index("row")
    layer = lax.axis_index("layer")
    core = lax.rem(me, 2)
    ax = lax.rem(me // 2, 2)
    ay = me // 4
    sib = ay * 4 + ax * 2 + 1 - core
    xn = ay * 4 + (1 - ax) * 2 + core
    yn = (1 - ay) * 4 + ax * 2 + core
    low, high = pl.ds(0, half), pl.ds(half, half)

    barrier = pltpu.get_barrier_semaphore()
    for to in (sib, xn, yn):
        pl.semaphore_signal(barrier, inc=1, device_id=(layer, to), device_id_type=MESH)
    for step in range(1, layers):
        pl.semaphore_signal(barrier, inc=1, device_id=(lax.rem(layer + step, layers), me), device_id_type=MESH)
    pl.semaphore_wait(barrier, 3 + layers - 1)

    def send(src, dst, sems, slot, to_layer, to):
        return pltpu.make_async_remote_copy(
            src_ref=src,
            dst_ref=dst,
            send_sem=sems.at[0, slot],
            recv_sem=sems.at[1, slot],
            device_id=(to_layer, to),
            device_id_type=MESH,
        )

    oy, ox = 1 - ay, 1 - ax
    chips = (oy * 2 + ox, ay * 2 + ox, oy * 2 + ax, ay * 2 + ax)
    started = []
    sib_copies = []
    for slot, chip in enumerate(chips):
        copy = send(p_ref.at[chip, 1 - core], from_sib.at[slot], sib_sem, slot, layer, sib)
        copy.start()
        sib_copies.append(copy)
    for slot, chip in enumerate(chips):
        sib_copies[slot].wait_recv()
        acc[slot] = p_ref[chip, core] + from_sib[slot]
        if slot == 0:
            x_far = send(acc.at[0, low], from_x.at[0], plane_sem, 0, layer, xn)
            y_far = send(acc.at[0, high], from_y.at[0], plane_sem, 1, layer, yn)
            x_far.start()
            y_far.start()
        if slot == 1:
            x_near = send(acc.at[1, low], from_x.at[1], plane_sem, 2, layer, xn)
            x_near.start()
        if slot == 2:
            y_near = send(acc.at[2, high], from_y.at[1], plane_sem, 3, layer, yn)
            y_near.start()
    x_far.wait_recv()
    mid_y[...] = acc[2, low] + from_x[0]
    y_end = send(mid_y, end_y, plane_sem, 4, layer, yn)
    y_end.start()
    y_far.wait_recv()
    mid_x[...] = acc[1, high] + from_y[0]
    x_end = send(mid_x, end_x, plane_sem, 5, layer, xn)
    x_end.start()
    x_near.wait_recv()
    y_near.wait_recv()
    y_end.wait_recv()
    x_end.wait_recv()
    total[low] = (acc[3, low] + from_x[1]) + end_y[...]
    total[high] = (acc[3, high] + from_y[1]) + end_x[...]
    started += sib_copies + [x_far, y_far, x_near, y_near, y_end, x_end]

    def part(at):
        return pl.ds(pl.multiple_of(at * piece, piece), piece)

    copies = []
    for step in range(1, layers):
        to = lax.rem(layer + step, layers)
        copy = send(total.at[part(to)], from_z.at[step - 1], z_sem, step - 1, to, me)
        copy.start()
        copies.append(copy)
    mine = total[part(layer)]
    for step in range(1, layers):
        copies[step - 1].wait_recv()
        mine = mine + from_z[step - 1]
    out_ref[part(layer)] = rhs_ref[part(layer)] - mine
    started += copies
    copies = []
    for step in range(1, layers):
        to = lax.rem(layer + step, layers)
        copy = send(out_ref.at[part(layer)], out_ref.at[part(layer)], z_sem, layers - 2 + step, to, me)
        copy.start()
        copies.append(copy)
    for step in range(1, layers):
        origin = lax.rem(layer + layers - step, layers)
        send(out_ref.at[part(origin)], out_ref.at[part(origin)], z_sem, layers - 2 + step, origin, me).wait_recv()
    for copy in started + copies:
        copy.wait_send()


def reduce_root(partial, rhs_root, layers, collective_id):
    depth, breadth = rhs_root.shape
    half = (depth // 2, breadth)
    return pl.pallas_call(
        functools.partial(reduce_kernel, layers),
        out_shape=jax.ShapeDtypeStruct((depth, breadth), F32),
        in_specs=[pl.BlockSpec(memory_space=pltpu.VMEM)] * 2,
        out_specs=pl.BlockSpec(memory_space=pltpu.VMEM),
        scratch_shapes=[
            pltpu.VMEM((4, depth, breadth), F32),
            pltpu.VMEM((4, depth, breadth), F32),
            pltpu.VMEM((2,) + half, F32),
            pltpu.VMEM((2,) + half, F32),
            pltpu.VMEM(half, F32),
            pltpu.VMEM(half, F32),
            pltpu.VMEM(half, F32),
            pltpu.VMEM(half, F32),
            pltpu.VMEM((depth, breadth), F32),
            pltpu.VMEM((layers - 1, depth // layers, breadth), F32),
            pltpu.SemaphoreType.DMA((2, 4)),
            pltpu.SemaphoreType.DMA((2, 6)),
            pltpu.SemaphoreType.DMA((2, 2 * (layers - 1))),
        ],
        compiler_params=pltpu.CompilerParams(
            collective_id=collective_id, has_side_effects=True, vmem_limit_bytes=16 << 20
        ),
    )(partial.reshape(4, 2, depth, breadth), rhs_root)


def fold(cube, matrices, piece, collective_id):
    if cube:
        return gather_multiply(matrices, piece, collective_id)
    whole = lax.all_gather(piece, "row", axis=1, tiled=True)
    return jnp.einsum("kij,kjr->kir", matrices, whole, precision=lax.Precision.HIGHEST)


def body(cube, layers, rhs_sub, rhs_root, lower_inv, upper_inv, coupling_low, coupling_up, tile_mask, root_inv):
    pattern = tile_mask[0]
    interim = fold(cube, lower_inv[0], rhs_sub[0], 1)
    partial = masked_low(coupling_low[0], pattern, interim)
    if cube and layers > 1:
        reduced = reduce_root(partial, rhs_root, layers, 5)
    else:
        partial = lax.psum_scatter(partial, "row", scatter_dimension=0, tiled=True)
        reduced = rhs_root - lax.psum(partial, "layer")
    sol_root = fold(cube, root_inv[None], reduced[None], 2)[0]
    if cube:
        whole = gather_only(sol_root, 3)
    else:
        whole = lax.all_gather(sol_root, "row", axis=0, tiled=True)
    residue = masked_up(coupling_up[0], pattern, whole, interim)
    solved = fold(cube, upper_inv[0], residue, 4)
    return solved[None], sol_root


def solution(mesh):
    return jax.shard_map(
        functools.partial(body, mesh.shape["row"] == CUBE, mesh.shape["layer"]),
        mesh=mesh,
        in_specs=(
            P("layer", None, "row", None),
            P("row", None),
            P("layer", None, "row", None),
            P("layer", None, "row", None),
            P("layer", None, None, "row"),
            P("layer", None, "row", None),
            P("layer", None, None, "row"),
            P("row", None),
        ),
        out_specs=(P("layer", None, "row", None), P("row", None)),
        check_vma=False,
    )
```

```python
import functools

import jax
import jax.numpy as jnp
from jax import lax
from jax.experimental import pallas as pl
from jax.experimental.pallas import tpu as pltpu
from jax.sharding import PartitionSpec as P

TILE = 128
CUBE = 8
PIECES = 2
MESH = pl.DeviceIdType.MESH
F32, BF16 = jnp.float32, jnp.bfloat16


def split(a):
    high = a.astype(BF16)
    return high, (a - high.astype(F32)).astype(BF16)


def dot3(a, b):
    ah, al = split(a)
    bh, bl = split(b)
    dot = functools.partial(jnp.dot, preferred_element_type=F32)
    return dot(ah, bh) + (dot(ah, bl) + dot(al, bh))


def gather_kernel(multiply, *refs):
    if multiply:
        x_ref, w_hbm, out_ref, held, weights, send_sem, recv_sem, w_sem = refs
    else:
        x_ref, out_ref, send_sem, recv_sem = refs
        held = out_ref
    count, depth, _ = x_ref.shape
    chunk = depth // PIECES
    half = chunk // 2
    me = lax.axis_index("row")
    layer = lax.axis_index("layer")
    core = lax.rem(me, 2)
    ax = lax.rem(me // 2, 2)
    ay = me // 4

    def place(fy, fx, fc):
        y = 1 - ay if fy else ay
        x = 1 - ax if fx else ax
        c = 1 - core if fc else core
        return y * 4 + x * 2 + c

    own, sib, xn, yn = place(0, 0, 0), place(0, 0, 1), place(0, 1, 0), place(1, 0, 0)
    diag, sx, sy, sd = place(1, 1, 0), place(0, 1, 1), place(1, 0, 1), place(1, 1, 1)

    barrier = pltpu.get_barrier_semaphore()
    for to in (sib, xn, yn):
        pl.semaphore_signal(barrier, inc=1, device_id=(layer, to), device_id_type=MESH)

    def weight_copy(k):
        return pltpu.make_async_copy(w_hbm.at[k], weights.at[k], w_sem.at[k])

    if multiply:
        for k in range(count):
            weight_copy(k).start()
    for k in range(count):
        held[k, own] = x_ref[k]
    pl.semaphore_wait(barrier, 3)

    every, low, high = (0, chunk), (0, half), (half, half)
    routes = (
        (own, every, sib),
        (own, every, xn),
        (own, every, yn),
        (xn, low, yn),
        (xn, every, sib),
        (yn, high, xn),
        (yn, every, sib),
        (diag, low, sib),
        (diag, high, sib),
    )

    def rows_of(k, span):
        offset = lax.rem(k, PIECES) * chunk + span[0]
        return pl.ds(pl.multiple_of(offset, half), span[1])

    def route(slot, k):
        block, span, to = routes[slot]
        ref = held.at[lax.div(k, PIECES), block, rows_of(k, span)]
        return pltpu.make_async_remote_copy(
            src_ref=ref,
            dst_ref=ref,
            send_sem=send_sem.at[slot, k],
            recv_sem=recv_sem.at[slot, k],
            device_id=(layer, to),
            device_id_type=MESH,
        )

    def meet(k, block):
        if multiply:
            at = lax.div(k, PIECES)
            offset = block * depth + lax.rem(k, PIECES) * chunk
            columns = pl.ds(pl.multiple_of(offset, chunk), chunk)
            out_ref[at] += dot3(weights[at, :, columns], held[at, block, rows_of(k, every)])

    for k in range(count * PIECES):
        for slot in (1, 2, 0):
            route(slot, k).start()

    def first(k, carry):
        if multiply:
            weight_copy(k).wait()
            columns = pl.ds(pl.multiple_of(own * depth, depth), depth)
            out_ref[k] = dot3(weights[k, :, columns], x_ref[k])
        return carry

    def second(k, carry):
        route(1, k).wait_recv()
        route(3, k).start()
        route(4, k).start()
        route(2, k).wait_recv()
        route(5, k).start()
        route(6, k).start()
        meet(k, xn)
        meet(k, yn)
        route(0, k).wait_recv()
        meet(k, sib)
        return carry

    def third(k, carry):
        route(3, k).wait_recv()
        route(7, k).start()
        route(5, k).wait_recv()
        route(8, k).start()
        route(4, k).wait_recv()
        meet(k, sx)
        route(6, k).wait_recv()
        meet(k, sy)
        meet(k, diag)
        route(7, k).wait_recv()
        route(8, k).wait_recv()
        meet(k, sd)
        return carry

    def last(k, carry):
        for slot in range(9):
            route(slot, k).wait_send()
        return carry

    lax.fori_loop(0, count, first, 0)
    for stage in (second, third, last):
        lax.fori_loop(0, count * PIECES, stage, 0)


def gather_multiply(matrices, piece, collective_id):
    count, rows, wide = matrices.shape
    _, depth, breadth = piece.shape
    return pl.pallas_call(
        functools.partial(gather_kernel, True),
        out_shape=jax.ShapeDtypeStruct((count, rows, breadth), F32),
        in_specs=[pl.BlockSpec(memory_space=pltpu.VMEM), pl.BlockSpec(memory_space=pl.ANY)],
        out_specs=pl.BlockSpec(memory_space=pltpu.VMEM),
        scratch_shapes=[
            pltpu.VMEM((count, CUBE, depth, breadth), F32),
            pltpu.VMEM((count, rows, wide), F32),
            pltpu.SemaphoreType.DMA((9, count * PIECES)),
            pltpu.SemaphoreType.DMA((9, count * PIECES)),
            pltpu.SemaphoreType.DMA((count,)),
        ],
        compiler_params=pltpu.CompilerParams(
            collective_id=collective_id, has_side_effects=True, vmem_limit_bytes=56 << 20
        ),
        cost_estimate=pl.CostEstimate(
            flops=6 * count * rows * wide * breadth, bytes_accessed=4 * matrices.size, transcendentals=0
        ),
    )(piece, matrices)


def gather_only(piece, collective_id):
    depth, breadth = piece.shape
    out = pl.pallas_call(
        functools.partial(gather_kernel, False),
        out_shape=jax.ShapeDtypeStruct((1, CUBE, depth, breadth), F32),
        in_specs=[pl.BlockSpec(memory_space=pltpu.VMEM)],
        out_specs=pl.BlockSpec(memory_space=pltpu.VMEM),
        scratch_shapes=[pltpu.SemaphoreType.DMA((9, PIECES)), pltpu.SemaphoreType.DMA((9, PIECES))],
        compiler_params=pltpu.CompilerParams(
            collective_id=collective_id, has_side_effects=True, vmem_limit_bytes=16 << 20
        ),
    )(piece[None])
    return out.reshape(CUBE * depth, breadth)


def low_kernel(c_ref, m_ref, x_ref, o_ref):
    k = pl.program_id(1)

    @pl.when(k == 0)
    def _():
        o_ref[...] = jnp.zeros_like(o_ref)

    for t in range(c_ref.shape[1] // TILE):
        rows = pl.ds(t * TILE, TILE)
        o_ref[rows, :] += dot3(c_ref[0, rows, :] * m_ref[0, t], x_ref[k])


def masked_low(coupling, pattern, interim):
    count, height, wide = coupling.shape
    breadth = interim.shape[2]
    block = min(512, height)
    weights = jnp.repeat(pattern.astype(F32), TILE, axis=2)[:, :, None, :]
    return pl.pallas_call(
        low_kernel,
        grid=(height // block, count),
        out_shape=jax.ShapeDtypeStruct((height, breadth), F32),
        in_specs=[
            pl.BlockSpec((1, block, wide), lambda i, k: (k, i, 0)),
            pl.BlockSpec((1, block // TILE, 1, wide), lambda i, k: (k, i, 0, 0)),
            pl.BlockSpec(interim.shape, lambda i, k: (0, 0, 0)),
        ],
        out_specs=pl.BlockSpec((block, breadth), lambda i, k: (i, 0)),
        compiler_params=pltpu.CompilerParams(vmem_limit_bytes=56 << 20),
    )(coupling, weights, interim)


def up_kernel(u_ref, m_ref, s_ref, i_ref, o_ref):
    for t in range(u_ref.shape[1] // TILE):
        rows = pl.ds(t * TILE, TILE)
        o_ref[0, rows, :] = i_ref[0, rows, :] - dot3(u_ref[0, rows, :] * m_ref[0, t], s_ref[...])


def masked_up(coupling, pattern, sol_root, interim):
    count, height, wide = coupling.shape
    breadth = sol_root.shape[1]
    block = min(256, height)
    weights = jnp.repeat(jnp.transpose(pattern, (0, 2, 1)).astype(F32), TILE, axis=2)[:, :, None, :]
    return pl.pallas_call(
        up_kernel,
        grid=(count, height // block),
        out_shape=jax.ShapeDtypeStruct((count, height, breadth), F32),
        in_specs=[
            pl.BlockSpec((1, block, wide), lambda k, i: (k, i, 0)),
            pl.BlockSpec((1, block // TILE, 1, wide), lambda k, i: (k, i, 0, 0)),
            pl.BlockSpec(sol_root.shape, lambda k, i: (0, 0)),
            pl.BlockSpec((1, block, breadth), lambda k, i: (k, i, 0)),
        ],
        out_specs=pl.BlockSpec((1, block, breadth), lambda k, i: (k, i, 0)),
        compiler_params=pltpu.CompilerParams(vmem_limit_bytes=56 << 20),
    )(coupling, weights, sol_root, interim)


def reduce_kernel(layers, p_ref, rhs_ref, out_ref, from_sib, acc, from_x, from_y, mid_x, mid_y, end_x, end_y, total, from_z,
                  sib_sem, plane_sem, z_sem):
    depth = rhs_ref.shape[0]
    half = depth // 2
    piece = depth // layers
    me = lax.axis_index("row")
    layer = lax.axis_index("layer")
    core = lax.rem(me, 2)
    ax = lax.rem(me // 2, 2)
    ay = me // 4
    sib = ay * 4 + ax * 2 + 1 - core
    xn = ay * 4 + (1 - ax) * 2 + core
    yn = (1 - ay) * 4 + ax * 2 + core
    low, high = pl.ds(0, half), pl.ds(half, half)

    barrier = pltpu.get_barrier_semaphore()
    for to in (sib, xn, yn):
        pl.semaphore_signal(barrier, inc=1, device_id=(layer, to), device_id_type=MESH)
    for step in range(1, layers):
        pl.semaphore_signal(barrier, inc=1, device_id=(lax.rem(layer + step, layers), me), device_id_type=MESH)
    pl.semaphore_wait(barrier, 3 + layers - 1)

    def send(src, dst, sems, slot, to_layer, to):
        return pltpu.make_async_remote_copy(
            src_ref=src,
            dst_ref=dst,
            send_sem=sems.at[0, slot],
            recv_sem=sems.at[1, slot],
            device_id=(to_layer, to),
            device_id_type=MESH,
        )

    oy, ox = 1 - ay, 1 - ax
    chips = (oy * 2 + ox, ay * 2 + ox, oy * 2 + ax, ay * 2 + ax)
    started = []
    sib_copies = []
    for slot, chip in enumerate(chips):
        copy = send(p_ref.at[chip, 1 - core], from_sib.at[slot], sib_sem, slot, layer, sib)
        copy.start()
        sib_copies.append(copy)
    for slot, chip in enumerate(chips):
        sib_copies[slot].wait_recv()
        acc[slot] = p_ref[chip, core] + from_sib[slot]
        if slot == 0:
            x_far = send(acc.at[0, low], from_x.at[0], plane_sem, 0, layer, xn)
            y_far = send(acc.at[0, high], from_y.at[0], plane_sem, 1, layer, yn)
            x_far.start()
            y_far.start()
        if slot == 1:
            x_near = send(acc.at[1, low], from_x.at[1], plane_sem, 2, layer, xn)
            x_near.start()
        if slot == 2:
            y_near = send(acc.at[2, high], from_y.at[1], plane_sem, 3, layer, yn)
            y_near.start()
    x_far.wait_recv()
    mid_y[...] = acc[2, low] + from_x[0]
    y_end = send(mid_y, end_y, plane_sem, 4, layer, yn)
    y_end.start()
    y_far.wait_recv()
    mid_x[...] = acc[1, high] + from_y[0]
    x_end = send(mid_x, end_x, plane_sem, 5, layer, xn)
    x_end.start()
    x_near.wait_recv()
    y_near.wait_recv()
    y_end.wait_recv()
    x_end.wait_recv()
    total[low] = (acc[3, low] + from_x[1]) + end_y[...]
    total[high] = (acc[3, high] + from_y[1]) + end_x[...]
    started += sib_copies + [x_far, y_far, x_near, y_near, y_end, x_end]

    def part(at):
        return pl.ds(pl.multiple_of(at * piece, piece), piece)

    copies = []
    for step in range(1, layers):
        to = lax.rem(layer + step, layers)
        copy = send(total.at[part(to)], from_z.at[step - 1], z_sem, step - 1, to, me)
        copy.start()
        copies.append(copy)
    mine = total[part(layer)]
    for step in range(1, layers):
        copies[step - 1].wait_recv()
        mine = mine + from_z[step - 1]
    out_ref[part(layer)] = rhs_ref[part(layer)] - mine
    started += copies
    copies = []
    for step in range(1, layers):
        to = lax.rem(layer + step, layers)
        copy = send(out_ref.at[part(layer)], out_ref.at[part(layer)], z_sem, layers - 2 + step, to, me)
        copy.start()
        copies.append(copy)
    for step in range(1, layers):
        origin = lax.rem(layer + layers - step, layers)
        send(out_ref.at[part(origin)], out_ref.at[part(origin)], z_sem, layers - 2 + step, origin, me).wait_recv()
    for copy in started + copies:
        copy.wait_send()


def reduce_root(partial, rhs_root, layers, collective_id):
    depth, breadth = rhs_root.shape
    half = (depth // 2, breadth)
    return pl.pallas_call(
        functools.partial(reduce_kernel, layers),
        out_shape=jax.ShapeDtypeStruct((depth, breadth), F32),
        in_specs=[pl.BlockSpec(memory_space=pltpu.VMEM)] * 2,
        out_specs=pl.BlockSpec(memory_space=pltpu.VMEM),
        scratch_shapes=[
            pltpu.VMEM((4, depth, breadth), F32),
            pltpu.VMEM((4, depth, breadth), F32),
            pltpu.VMEM((2,) + half, F32),
            pltpu.VMEM((2,) + half, F32),
            pltpu.VMEM(half, F32),
            pltpu.VMEM(half, F32),
            pltpu.VMEM(half, F32),
            pltpu.VMEM(half, F32),
            pltpu.VMEM((depth, breadth), F32),
            pltpu.VMEM((layers - 1, depth // layers, breadth), F32),
            pltpu.SemaphoreType.DMA((2, 4)),
            pltpu.SemaphoreType.DMA((2, 6)),
            pltpu.SemaphoreType.DMA((2, 2 * (layers - 1))),
        ],
        compiler_params=pltpu.CompilerParams(
            collective_id=collective_id, has_side_effects=True, vmem_limit_bytes=16 << 20
        ),
    )(partial.reshape(4, 2, depth, breadth), rhs_root)


def fold(cube, matrices, piece, collective_id):
    if cube:
        return gather_multiply(matrices, piece, collective_id)
    whole = lax.all_gather(piece, "row", axis=1, tiled=True)
    return jnp.einsum("kij,kjr->kir", matrices, whole, precision=lax.Precision.HIGHEST)


def body(cube, layers, rhs_sub, rhs_root, lower_inv, upper_inv, coupling_low, coupling_up, tile_mask, root_inv):
    pattern = tile_mask[0]
    interim = fold(cube, lower_inv[0], rhs_sub[0], 1)
    partial = masked_low(coupling_low[0], pattern, interim)
    if cube and layers > 1:
        reduced = reduce_root(partial, rhs_root, layers, 5)
    else:
        partial = lax.psum_scatter(partial, "row", scatter_dimension=0, tiled=True)
        reduced = rhs_root - lax.psum(partial, "layer")
    sol_root = fold(cube, root_inv[None], reduced[None], 2)[0]
    if cube:
        whole = gather_only(sol_root, 3)
    else:
        whole = lax.all_gather(sol_root, "row", axis=0, tiled=True)
    residue = masked_up(coupling_up[0], pattern, whole, interim)
    solved = fold(cube, upper_inv[0], residue, 4)
    return solved[None], sol_root


def solution(mesh):
    return jax.shard_map(
        functools.partial(body, mesh.shape["row"] == CUBE, mesh.shape["layer"]),
        mesh=mesh,
        in_specs=(
            P("layer", None, "row", None),
            P("row", None),
            P("layer", None, "row", None),
            P("layer", None, "row", None),
            P("layer", None, None, "row"),
            P("layer", None, "row", None),
            P("layer", None, None, "row"),
            P("row", None),
        ),
        out_specs=(P("layer", None, "row", None), P("row", None)),
        check_vma=False,
    )
```
